32 devices in a mesh: video: 4 (over y, x), seq: 8 (over z, core).
Axes of the slice: x: 2, y: 2, z: 4, core: 2. Of those that a mesh axis runs over, the one named last changes fastest.
Arguments:
- queries: bfloat16 [4096, 2048], P(('video', 'seq')), parts along dimension 0, may hold values from -80 to 80
- keys: bfloat16 [4096, 2048], P(('video', 'seq')), parts along dimension 0, may hold values from -5 to 5
- values: bfloat16 [4096, 2048], P(('video', 'seq')), parts along dimension 0, may hold values from -6 to 6
- history: bfloat16 [16, 2048], P(None, ('video', 'seq')), parts along dimension 1, may hold values from -6 to 6
- levels: int32 [32], P('video'), parts along dimension 0, may hold values from 2 to 16, as said below
- patch_two: bfloat16 [32, 3072], replicated, may hold values from -1 to 1
- patch_four: bfloat16 [64, 3072], replicated, may hold values from -0.75 to 0.75
- patch_sixteen: bfloat16 [256, 3072], replicated, may hold values from -0.375 to 0.375
- mod_scale: float32 [3072], replicated, may hold values from -0.5 to 0.5
- mod_shift: float32 [3072], replicated, may hold values from -4 to 4
- kv_weight: bfloat16 [3072, 4096], P(None, 'seq'), may hold values from -0.109375 to 0.109375
- key_gain: float32 [128], replicated, may hold values from 0.5 to 2
Outputs:
- attended: bfloat16 [4096, 2048], P(('video', 'seq')), parts along dimension 0
The draws below stay inside these ranges and needn't reach their ends.
There are 4 independent parts, one for each index of `video`. The reference program is written for one: setup_inputs(seed, part) draws one part's arguments, and reference() takes and returns one part's arrays. A program takes and returns all parts, laid end to end along the dimension named above; an argument that names none is the same for every part. Nothing has to cross between parts.
Inputs may be any that keep to these rules, and one draw needn't show every extreme that they name: `levels`: each aligned group of four devices holds the factors 2, 4, 4 and 16 in some order, so that one device's block gives at most 32 history tokens.
All inputs are finite; a program needn't handle non-finite values.
Results may differ from the reference program's by a relative error of at most 0.0034.
Values may be sent and summed in bfloat16 or wider, within the bound.
A program may use at most 128 MiB of HBM per device.

```python
import math
import jax
import jax.numpy as jnp
from jax import lax

D = 3072
HEADS = 16
HD = 128
LATC = 16
HPOS = 64
TOKENS = 1024
HIST = 136
N_SEQ = 8


def paired_rows(key):
    base = jax.random.fold_in(key, 7)
    first, second = jax.random.split(base, 2)
    width = HEADS * HD
    key_rows = jnp.clip(jax.random.normal(first, (TOKENS, width), jnp.float32), -4.0, 4.0)
    query_rows = jnp.clip(jax.random.normal(second, (TOKENS, width), jnp.float32), -4.0, 4.0)
    return (query_rows, key_rows)


def draw_queries(key, part):
    return paired_rows(key)[0].astype(jnp.bfloat16)


def draw_keys(key, part):
    return paired_rows(key)[1].astype(jnp.bfloat16)


def draw_levels(key, part):
    base = jax.random.fold_in(key, 11)
    groups = N_SEQ // 4
    scores = jax.random.randint(base, (groups, 4), 0, 1 << 20) * 4 + jnp.arange(4, dtype=jnp.int32)[None, :]
    order = jnp.argsort(scores, axis=1)
    table = jnp.array([2, 4, 4, 16], jnp.int32)
    return table[order].reshape(N_SEQ).astype(jnp.int32)


def block_scale(key, extent, pieces, low, top_value):
    loudness = 1.0
    for axis_at, parts in pieces:
        draws = jax.random.uniform(jax.random.fold_in(jax.random.fold_in(key, 6), axis_at), (parts,), jnp.float32, low / len(pieces), top_value / len(pieces))
        loudness = loudness * jnp.repeat(jnp.exp(draws), extent[axis_at] // parts).reshape((-1,) + (1,) * (len(extent) - 1 - axis_at))
    return loudness


def centred(stream_key, dims, scale, limit, cuts=(), kind=jnp.bfloat16):
    gain = block_scale(stream_key, dims, cuts, -0.22, 0.18) if cuts else 1.0
    values = jax.random.normal(stream_key, dims, jnp.float32) * scale * gain
    return jnp.minimum(jnp.maximum(values, -limit), limit).astype(kind)


def setup_inputs(seed: int = 0, part: int = 0) -> dict:
    splits = jax.random.split(jax.random.key(seed), 13)
    part_splits = jax.random.split(jax.random.fold_in(splits[12], part), 13)
    queries = draw_queries(jax.random.fold_in(jax.random.fold_in(splits[12], part), 71), part)
    keys = draw_keys(jax.random.fold_in(jax.random.fold_in(splits[12], part), 71), part)
    values = centred(part_splits[2], (TOKENS, HEADS * HD), 1.0, 6.0, ((0, 8),))
    history = centred(part_splits[3], (LATC, HPOS * N_SEQ), 1.0, 6.0, ((1, 8),))
    levels = draw_levels(jax.random.fold_in(jax.random.fold_in(splits[12], part), 71), part)
    patch_two = centred(splits[5], (2 * LATC, D), (2 * LATC) ** -0.5, 1.0)
    patch_four = centred(splits[6], (4 * LATC, D), (4 * LATC) ** -0.5, 0.75)
    patch_sixteen = centred(splits[7], (16 * LATC, D), (16 * LATC) ** -0.5, 0.375)
    mod_scale = jnp.clip(jax.random.uniform(splits[8], (D,), jnp.float32, -0.5, 0.5), -0.5, 0.5)
    mod_shift = centred(splits[9], (D,), 1.0, 4.0, (), jnp.float32)
    kv_weight = centred(splits[10], (D, 2 * HEADS * HD), D ** -0.5, 0.109375, ((1, 8),))
    key_gain = jnp.clip(jnp.exp(jax.random.uniform(splits[11], (HD,), jnp.float32, math.log(0.5), math.log(2.0))), 0.5, 2.0)
    return {"queries": queries, "keys": keys, "values": values, "history": history, "levels": levels, "patch_two": patch_two, "patch_four": patch_four, "patch_sixteen": patch_sixteen, "mod_scale": mod_scale, "mod_shift": mod_shift, "kv_weight": kv_weight, "key_gain": key_gain}


EPS = 1e-06

def level_tokens(history, weight, level):
    width = history.shape[1]
    grouped = history.reshape(LATC, width // level, level).transpose(1, 0, 2).reshape(width // level, LATC * level)
    return jnp.dot(grouped, weight, preferred_element_type=jnp.float32).astype(jnp.bfloat16)

def reference(queries, keys, values, history, levels, patch_two, patch_four, patch_sixteen, mod_scale, mod_shift, kv_weight, key_gain):
    counts = (HPOS // levels).astype(jnp.int32)
    ends = jnp.cumsum(counts).astype(jnp.int32)
    starts = ends - counts
    place = jnp.arange(HIST, dtype=jnp.int32)
    owner = lax.optimization_barrier(jnp.sum((ends[None, :] <= place[:, None]).astype(jnp.int32), axis=1)).astype(jnp.int32)
    inner = (place - starts[owner]).astype(jnp.int32)
    level = levels[owner]
    tokens_two = level_tokens(history, patch_two, 2)
    tokens_four = level_tokens(history, patch_four, 4)
    tokens_sixteen = level_tokens(history, patch_sixteen, 16)
    pick_two = jnp.take(tokens_two, (owner * (HPOS // 2) + jnp.minimum(inner, HPOS // 2 - 1)).astype(jnp.int32), axis=0)
    pick_four = jnp.take(tokens_four, (owner * (HPOS // 4) + jnp.minimum(inner, HPOS // 4 - 1)).astype(jnp.int32), axis=0)
    pick_sixteen = jnp.take(tokens_sixteen, (owner * (HPOS // 16) + jnp.minimum(inner, HPOS // 16 - 1)).astype(jnp.int32), axis=0)
    hidden = jnp.where((level == 2)[:, None], pick_two, jnp.where((level == 4)[:, None], pick_four, pick_sixteen))
    feats = hidden.astype(jnp.float32)
    mean = lax.optimization_barrier(jnp.mean(feats, axis=1, keepdims=True))
    centered = feats - mean
    var = lax.optimization_barrier(jnp.mean(centered * centered, axis=1, keepdims=True))
    normed = (centered * lax.rsqrt(var + EPS) * (1.0 + mod_scale) + mod_shift).astype(jnp.bfloat16)
    history_kv = jnp.dot(normed, kv_weight, preferred_element_type=jnp.float32).astype(jnp.bfloat16)
    pairs = history_kv.reshape(HIST, HD, 2, HEADS).transpose(0, 3, 2, 1)
    first = pairs[:, :, 0, :].astype(jnp.float32)
    history_keys = (first * lax.rsqrt(lax.optimization_barrier(jnp.mean(first * first, axis=-1, keepdims=True)) + EPS) * key_gain).astype(jnp.bfloat16)
    history_values = pairs[:, :, 1, :]
    scale = HD ** (-0.5)

    def one_head(item):
        query, key_part, value_part, hist_key, hist_value = item
        all_keys = jnp.concatenate([key_part, hist_key], axis=0)
        all_values = jnp.concatenate([value_part, hist_value], axis=0)
        scores = jnp.dot(query, all_keys.T, preferred_element_type=jnp.float32) * scale
        top = lax.optimization_barrier(jnp.max(scores, axis=1, keepdims=True))
        weights = jnp.exp(scores - top)
        total = lax.optimization_barrier(jnp.sum(weights, axis=1, keepdims=True))
        probs = weights.astype(jnp.bfloat16)
        mixed = jnp.dot(probs, all_values, preferred_element_type=jnp.float32) / total
        return mixed.astype(jnp.bfloat16)
    split_q = queries.reshape(TOKENS, HEADS, HD).transpose(1, 0, 2)
    split_k = keys.reshape(TOKENS, HEADS, HD).transpose(1, 0, 2)
    split_v = values.reshape(TOKENS, HEADS, HD).transpose(1, 0, 2)
    result = lax.map(one_head, (split_q, split_k, split_v, history_keys.transpose(1, 0, 2), history_values.transpose(1, 0, 2)))
    return result.transpose(1, 0, 2).reshape(TOKENS, HEADS * HD)
```

```python
import functools

import jax
import jax.numpy as jnp
from jax import lax
from jax.experimental import pallas as pl
from jax.experimental.pallas import tpu as pltpu
from jax.sharding import PartitionSpec as P

EPS = 1e-06


def divisor_near(total, target):
    parts = max(1, -(-total // target))
    while total % parts != 0:
        parts += 1
    return parts


def key_normed(pairs, gain):
    first = pairs[..., 0, :].astype(jnp.float32)
    scaled = first * lax.rsqrt(jnp.mean(first * first, axis=-1, keepdims=True) + EPS) * gain
    return jnp.concatenate([scaled.astype(jnp.bfloat16), pairs[..., 1, :]], axis=-1)


def level_tokens(everything, weight, level):
    channels, width = everything.shape
    grouped = (
        everything.reshape(channels, width // level, level)
        .transpose(1, 0, 2)
        .reshape(width // level, channels * level)
    )
    return jnp.dot(grouped, weight, preferred_element_type=jnp.float32).astype(jnp.bfloat16)


def history_rows(levels, positions):
    groups = levels.shape[0]
    counts = positions // levels
    before = jnp.arange(groups)[None, :] <= jnp.arange(groups)[:, None]
    ends = jnp.sum(jnp.where(before, counts[None, :], 0), axis=1)
    starts = ends - counts
    block_ids = jnp.arange(groups, dtype=jnp.int32)
    rows_total = 17 * positions * groups // 64
    place = jnp.arange(rows_total, dtype=jnp.int32)
    owner = jnp.sum((ends[None, :] <= place[:, None]).astype(jnp.int32), axis=1)
    match = owner[:, None] == block_ids[None, :]
    inner = place - jnp.sum(jnp.where(match, starts[None, :], 0), axis=1)
    live = jnp.ones((rows_total,), bool)
    level = jnp.sum(jnp.where(match, levels[None, :], 0), axis=1)
    return (owner, inner, level, live)


def attend(query, sec_keys, sec_values, hist_keys, hist_values, live, scale):
    count, size = query.shape
    sources, each, _ = sec_keys.shape
    key_parts = divisor_near(sources, max(1, 2048 // each))
    key_blocks = sec_keys.reshape(key_parts, sources // key_parts * each, size)
    value_blocks = sec_values.reshape(key_parts, sources // key_parts * each, size)
    query_parts = divisor_near(count, 512)
    query_blocks = query.reshape(query_parts, count // query_parts, size)

    def one_block(block):
        scores = jnp.dot(block, hist_keys.T, preferred_element_type=jnp.float32) * scale
        scores = jnp.where(live[None, :], scores, -1e30)
        top = jnp.max(scores, axis=1, keepdims=True)
        weights = jnp.where(live[None, :], jnp.exp(scores - top), 0.0)
        total = jnp.sum(weights, axis=1, keepdims=True)
        acc = jnp.dot(weights.astype(jnp.bfloat16), hist_values, preferred_element_type=jnp.float32)

        def step(carry, pair):
            top_now, total_now, acc_now = carry
            key_block, value_block = pair
            fresh = jnp.dot(block, key_block.T, preferred_element_type=jnp.float32) * scale
            newer = jnp.maximum(top_now, jnp.max(fresh, axis=1, keepdims=True))
            fade = jnp.exp(top_now - newer)
            weights_now = jnp.exp(fresh - newer)
            total_next = total_now * fade + jnp.sum(weights_now, axis=1, keepdims=True)
            acc_next = acc_now * fade + jnp.dot(
                weights_now.astype(jnp.bfloat16), value_block, preferred_element_type=jnp.float32
            )
            return ((newer, total_next, acc_next), None)

        (top, total, acc), _ = lax.scan(step, (top, total, acc), (key_blocks, value_blocks))
        return (acc / total).astype(jnp.bfloat16)

    return lax.map(one_block, query_blocks).reshape(count, size)


def shards(
    queries,
    keys,
    values,
    history,
    levels,
    patch_two,
    patch_four,
    patch_sixteen,
    mod_scale,
    mod_shift,
    kv_weight,
    key_gain,
):
    groups = lax.axis_size("seq")
    device = lax.axis_index("seq")
    tok_dev, width = queries.shape
    head_dim = key_gain.shape[0]
    heads = width // head_dim
    q_split = max(groups // heads, 1)
    per_group = max(heads // groups, 1)
    head_groups = heads // per_group
    q_rows = tok_dev // q_split
    positions = history.shape[1]
    scale = head_dim ** (-0.5)
    everything = lax.all_gather(history, "seq", axis=1, tiled=True)
    owner, inner, level, live = history_rows(levels, positions)
    tokens_two = level_tokens(everything, patch_two, 2)
    tokens_four = level_tokens(everything, patch_four, 4)
    tokens_sixteen = level_tokens(everything, patch_sixteen, 16)
    rows_total = owner.shape[0]
    row_parts = divisor_near(rows_total, 512)

    def project(index):
        own, inn, lev = index
        pick_two = jnp.take(
            tokens_two, own * (positions // 2) + jnp.minimum(inn, positions // 2 - 1), axis=0
        )
        pick_four = jnp.take(
            tokens_four, own * (positions // 4) + jnp.minimum(inn, positions // 4 - 1), axis=0
        )
        pick_sixteen = jnp.take(
            tokens_sixteen, own * (positions // 16) + jnp.minimum(inn, positions // 16 - 1), axis=0
        )
        hidden = jnp.where(
            (lev == 2)[:, None], pick_two, jnp.where((lev == 4)[:, None], pick_four, pick_sixteen)
        )
        feats = hidden.astype(jnp.float32)
        mean = jnp.mean(feats, axis=1, keepdims=True)
        centered = feats - mean
        var = jnp.mean(centered * centered, axis=1, keepdims=True)
        normed = (centered * lax.rsqrt(var + EPS) * (1.0 + mod_scale) + mod_shift).astype(
            jnp.bfloat16
        )
        return jnp.dot(normed, kv_weight, preferred_element_type=jnp.float32).astype(jnp.bfloat16)

    share = lax.map(
        project,
        (owner.reshape(row_parts, -1), inner.reshape(row_parts, -1), level.reshape(row_parts, -1)),
    )
    share = share.reshape(rows_total, kv_weight.shape[1])
    pairs = jnp.concatenate(
        [
            keys.reshape(tok_dev, head_groups, per_group, head_dim),
            values.reshape(tok_dev, head_groups, per_group, head_dim),
        ],
        axis=-1,
    )
    full = lax.all_gather(share, "seq", axis=1, tiled=True)
    ordered = full.reshape(rows_total, head_dim, 2, heads).transpose(0, 3, 2, 1)
    mine = lax.dynamic_index_in_dim(
        ordered.reshape(rows_total, head_groups, per_group, 2, head_dim),
        device // q_split,
        axis=1,
        keepdims=False,
    )
    history_kv = key_normed(mine, key_gain)
    rows_each = pairs.shape[0]
    outgoing = jnp.broadcast_to(
        pairs.transpose(1, 0, 2, 3)[:, None],
        (head_groups, q_split, rows_each, per_group, 2 * head_dim),
    )
    outgoing = outgoing.reshape(groups, rows_each, per_group * 2 * head_dim)
    sending = (
        queries.reshape(q_split, q_rows, head_groups, per_group * head_dim)
        .transpose(2, 0, 1, 3)
        .reshape(groups, q_rows, per_group * head_dim)
    )
    got_queries, got_pairs = (
        lax.all_to_all(sending, "seq", split_axis=0, concat_axis=0, tiled=True),
        lax.all_to_all(outgoing, "seq", split_axis=0, concat_axis=0, tiled=True),
    )
    results = []
    for item in range(per_group):
        query = got_queries[:, :, item * head_dim : (item + 1) * head_dim].reshape(
            groups * q_rows, head_dim
        )
        base = item * 2 * head_dim
        sec_keys = got_pairs[:, :, base : base + head_dim]
        sec_values = got_pairs[:, :, base + head_dim : base + 2 * head_dim]
        hist_keys = history_kv[:, item, :head_dim]
        hist_values = history_kv[:, item, head_dim:]
        results.append(attend(query, sec_keys, sec_values, hist_keys, hist_values, live, scale))
    mixed = jnp.concatenate(results, axis=-1).reshape(groups, q_rows, per_group * head_dim)
    returned = lax.all_to_all(mixed, "seq", split_axis=0, concat_axis=0, tiled=True)
    return (
        returned.reshape(head_groups, q_split, q_rows, per_group * head_dim)
        .transpose(1, 2, 0, 3)
        .reshape(tok_dev, width)
    )


def joint_kernel(
    dims,
    levels_ref,
    history_ref,
    scale_ref,
    shift_ref,
    gain_ref,
    queries_ref,
    keys_ref,
    values_ref,
    two_ref,
    four_ref,
    sixteen_ref,
    weight_ref,
    out_ref,
    raw,
    patches,
    weight,
    spread,
    hidden,
    share_out,
    share_in,
    qbuf,
    kbuf,
    vbuf,
    obuf,
    load_sem,
    own_sem,
    hist_send,
    hist_recv,
    share_send,
    share_recv,
    kv_send,
    kv_recv,
    q_send,
    q_recv,
    o_send,
    o_recv,
):
    n, per, hd, rows, padded, positions, channels, off4, off16 = dims
    tok = queries_ref.shape[0]
    wide = per * hd
    half = padded // 2
    heads = n * per
    chan = hd // n
    kinds = 2 * per
    model = hidden.shape[1]
    bf, f32 = jnp.bfloat16, jnp.float32
    me = lax.axis_index("seq")

    def partner(i):
        return n // 2 + (1 - 2 * (i % 2)) * (i // 2)

    def target(i):
        return lax.rem(me + partner(i), n)

    def origin(i):
        return lax.rem(me + n - partner(i), n)

    def lanes(index):
        return pl.ds(pl.multiple_of(index * wide, 128), wide)

    def band(index):
        return pl.ds(pl.multiple_of(index * tok, 16), tok)

    def remote(src, dst, send, recv, device):
        return pltpu.make_async_remote_copy(
            src_ref=src,
            dst_ref=dst,
            send_sem=send,
            recv_sem=recv,
            device_id={"seq": device},
            device_id_type=pl.DeviceIdType.MESH,
        )

    def hist_copy(device, source):
        return remote(
            raw.at[source], raw.at[source], hist_send.at[device], hist_recv.at[source], device
        )

    def key_copy(device, source):
        return remote(
            keys_ref.at[:, lanes(device)],
            kbuf.at[band(source), :],
            kv_send.at[0, device],
            kv_recv.at[0, source],
            device,
        )

    def value_copy(device, source):
        return remote(
            values_ref.at[:, lanes(device)],
            vbuf.at[band(source), :],
            kv_send.at[1, device],
            kv_recv.at[1, source],
            device,
        )

    def query_copy(device, source):
        return remote(
            queries_ref.at[:, lanes(device)],
            qbuf.at[source],
            q_send.at[device],
            q_recv.at[source],
            device,
        )

    def share_copy(device, source):
        return remote(
            share_out.at[device],
            share_in.at[source],
            share_send.at[device],
            share_recv.at[source],
            device,
        )

    def out_copy(device, source):
        return remote(
            obuf.at[device],
            out_ref.at[:, lanes(source)],
            o_send.at[device],
            o_recv.at[source],
            device,
        )

    n2, n4, n16 = two_ref.shape[0], four_ref.shape[0], sixteen_ref.shape[0]
    loads = [
        pltpu.make_async_copy(two_ref, patches.at[pl.ds(0, n2), :], load_sem.at[0]),
        pltpu.make_async_copy(four_ref, patches.at[pl.ds(off4, n4), :], load_sem.at[1]),
        pltpu.make_async_copy(sixteen_ref, patches.at[pl.ds(off16, n16), :], load_sem.at[2]),
        pltpu.make_async_copy(weight_ref, weight, load_sem.at[3]),
    ]
    own = [
        pltpu.make_async_copy(keys_ref.at[:, lanes(me)], kbuf.at[band(me), :], own_sem.at[0]),
        pltpu.make_async_copy(values_ref.at[:, lanes(me)], vbuf.at[band(me), :], own_sem.at[1]),
        pltpu.make_async_copy(queries_ref.at[:, lanes(me)], qbuf.at[me], own_sem.at[2]),
    ]

    barrier = pltpu.get_barrier_semaphore()

    @pl.loop(1, n)
    def _(i):
        pl.semaphore_signal(
            barrier, inc=1, device_id={"seq": target(i)}, device_id_type=pl.DeviceIdType.MESH
        )

    for copy in loads + own:
        copy.start()
    gap = off16 - off4 - n4
    if gap:
        patches[off4 + n4 : off16, :] = jnp.zeros((gap, model), bf)
    raw[me] = jnp.concatenate(
        [history_ref[...], jnp.zeros((channels, 128 - positions), bf)], axis=1
    )
    pl.semaphore_wait(barrier, n - 1)

    @pl.loop(1, n)
    def _(i):
        hist_copy(target(i), me).start()

    @pl.loop(1, n)
    def _(i):
        key_copy(target(i), me).start()
        value_copy(target(i), me).start()

    spots = n * positions
    row = lax.broadcasted_iota(jnp.int32, (padded, spots), 0)
    spot = lax.broadcasted_iota(jnp.int32, (1, spots), 1)
    start = jnp.int32(0)
    first = jnp.zeros((1, spots), jnp.int32)
    factor = jnp.ones((1, spots), jnp.int32)
    block_levels = []
    for b in range(n):
        level = levels_ref[b]
        block_levels.append(level)
        inside = spot // positions == b
        first = jnp.where(inside, start, first)
        factor = jnp.where(inside, level, factor)
        start = start + jnp.where(
            level == 2, positions // 2, jnp.where(level == 4, positions // 4, positions // 16)
        )
    begin = (row - first) * factor
    local = spot % positions
    member = jnp.where((begin <= local) & (local < begin + factor), 1.0, 0.0).astype(bf)

    width = patches.shape[0]
    column = lax.broadcasted_iota(jnp.int32, (1, width), 1)
    kind = jnp.where(
        column < off4,
        2,
        jnp.where(column < off4 + n4, 4, jnp.where(column < off16, 1, 16)),
    )
    base = jnp.where(column < off4, 0, jnp.where(column < off16, off4, off16))
    within = column - base
    owner_channel = jnp.where(
        kind == 2, within // 2, jnp.where(kind == 4, within // 4, within // 16)
    )
    phase = within - owner_channel * kind
    channel = lax.broadcasted_iota(jnp.int32, (channels, width), 0)
    expand = jnp.where((channel == owner_channel) & (kind > 1), 1.0, 0.0).astype(bf)
    at = lax.broadcasted_iota(jnp.int32, (128, width), 0)
    remainder = jnp.where(kind == 2, at % 2, jnp.where(kind == 4, at % 4, at % 16))
    fits = remainder == phase

    @pl.loop(1, n)
    def _(i):
        hist_copy(origin(i), origin(i)).wait_recv()

    for b in range(n):
        spreaded = lax.dot_general(
            raw[b], expand, (((0,), (0,)), ((), ())), preferred_element_type=f32
        )
        keep = fits & (kind == block_levels[b])
        spread[b * positions : (b + 1) * positions, :] = jnp.where(keep, spreaded, 0.0).astype(bf)[
            :positions
        ]
    grouped = jnp.dot(member, spread[...], preferred_element_type=f32).astype(bf)
    for copy in loads[:3]:
        copy.wait()
    step = 512 if model % 512 == 0 else model
    total = jnp.zeros((padded, 1), f32)
    for c in range(0, model, step):
        tokens = jnp.dot(
            grouped, patches[:, c : c + step], preferred_element_type=f32
        ).astype(bf)
        hidden[:, c : c + step] = tokens
        total = total + jnp.sum(tokens.astype(f32), axis=1, keepdims=True)
    mean = total / model
    square = jnp.zeros((padded, 1), f32)
    for c in range(0, model, step):
        centered = hidden[:, c : c + step].astype(f32) - mean
        square = square + jnp.sum(centered * centered, axis=1, keepdims=True)
    inverse = lax.rsqrt(square / model + EPS)
    loads[3].wait()
    projected = jnp.zeros((padded, weight.shape[1]), f32)
    for c in range(0, model, step):
        centered = hidden[:, c : c + step].astype(f32) - mean
        normed = (
            centered * inverse * (1.0 + scale_ref[:, c : c + step]) + shift_ref[:, c : c + step]
        ).astype(bf)
        projected = projected + jnp.dot(
            normed, weight[c : c + step, :], preferred_element_type=f32
        )
    share = projected.astype(bf)

    cols = chan * 2 * heads
    take = lax.broadcasted_iota(jnp.int32, (cols, n * 128), 0)
    give = lax.broadcasted_iota(jnp.int32, (1, n * 128), 1)
    lane = give % (kinds * chan)
    dest = give // 128
    which = lane // chan
    wanted = (lane % chan) * 2 * heads + (which // per) * heads + dest * per + which % per
    order = jnp.where(take == wanted, 1.0, 0.0).astype(bf)
    low = jnp.dot(share[:half], order, preferred_element_type=f32)
    high = jnp.dot(share[half:], order, preferred_element_type=f32)
    both = jnp.where(give % 128 < kinds * chan, low, high).astype(bf)
    for g in range(n):
        share_out[g] = both[:, g * 128 : (g + 1) * 128]

    @pl.loop(1, n)
    def _(i):
        share_copy(target(i), me).start()

    @pl.loop(1, n)
    def _(i):
        query_copy(target(i), me).start()

    share_in[me] = share_out[me]
    taking = lax.broadcasted_iota(jnp.int32, (128, kinds * hd), 0)
    giving = lax.broadcasted_iota(jnp.int32, (1, kinds * hd), 1)
    in_head = giving % hd
    lane_of = (giving // hd) * chan + in_head % chan

    @pl.loop(1, n)
    def _(i):
        share_copy(origin(i), origin(i)).wait_recv()

    low = jnp.zeros((half, kinds * hd), f32)
    high = jnp.zeros((half, kinds * hd), f32)
    for s in range(n):
        from_s = in_head // chan == s
        put_low = jnp.where((taking == lane_of) & from_s, 1.0, 0.0).astype(bf)
        put_high = jnp.where((taking == lane_of + kinds * chan) & from_s, 1.0, 0.0).astype(bf)
        low = low + jnp.dot(share_in[s], put_low, preferred_element_type=f32)
        high = high + jnp.dot(share_in[s], put_high, preferred_element_type=f32)
    gathered = jnp.concatenate([low, high], axis=0)
    section = n * tok
    for h in range(per):
        key = gathered[:, h * hd : (h + 1) * hd]
        norm = lax.rsqrt(jnp.mean(key * key, axis=1, keepdims=True) + EPS)
        kbuf[section:, h * hd : (h + 1) * hd] = (key * norm * gain_ref[...]).astype(bf)
        vbuf[section:, h * hd : (h + 1) * hd] = gathered[
            :, (per + h) * hd : (per + h + 1) * hd
        ].astype(bf)

    for copy in own:
        copy.wait()

    @pl.loop(1, n)
    def _(i):
        key_copy(origin(i), origin(i)).wait_recv()
        value_copy(origin(i), origin(i)).wait_recv()

    rate = hd**-0.5 * 1.4426950408889634
    live = lax.broadcasted_iota(jnp.int32, (1, padded), 1) < rows
    across = (((1,), (1,)), ((), ()))

    def attend_block(source):
        for h in range(per):
            cut = slice(h * hd, (h + 1) * hd)
            query = qbuf[source, :, cut]
            near = lax.dot_general(query, kbuf[:section, cut], across, preferred_element_type=f32)
            past = lax.dot_general(query, kbuf[section:, cut], across, preferred_element_type=f32)
            past = jnp.where(live, past, -1e30)
            top = jnp.maximum(
                jnp.max(near, axis=1, keepdims=True), jnp.max(past, axis=1, keepdims=True)
            )
            near = jnp.exp2((near - top) * rate)
            past = jnp.exp2((past - top) * rate)
            total = jnp.sum(near, axis=1, keepdims=True) + jnp.sum(past, axis=1, keepdims=True)
            mixed = jnp.dot(near.astype(bf), vbuf[:section, cut], preferred_element_type=f32)
            mixed = mixed + jnp.dot(past.astype(bf), vbuf[section:, cut], preferred_element_type=f32)
            obuf[source, :, cut] = (mixed / total).astype(bf)

    attend_block(me)
    own_out = pltpu.make_async_copy(obuf.at[me], out_ref.at[:, lanes(me)], own_sem.at[3])
    own_out.start()

    @pl.loop(1, n)
    def _(i):
        source = origin(i)
        query_copy(source, source).wait_recv()
        attend_block(source)
        out_copy(source, me).start()

    @pl.loop(1, n)
    def _(i):
        device = target(i)
        hist_copy(device, me).wait_send()
        key_copy(device, me).wait_send()
        value_copy(device, me).wait_send()
        share_copy(device, me).wait_send()
        query_copy(device, me).wait_send()
        out_copy(device, me).wait_send()

    @pl.loop(1, n)
    def _(i):
        out_copy(origin(i), origin(i)).wait_recv()

    own_out.wait()


def fits_kernel(groups, tok_dev, width, head_dim, positions):
    heads = width // head_dim
    if groups < 2 or groups % 2 or heads % groups or head_dim % groups or tok_dev % 16:
        return False
    per_group = heads // groups
    held = 4 * 2 * groups * tok_dev * per_group * head_dim
    lanes = 4 * per_group * (head_dim // groups)
    return held <= 16 * 2**20 and lanes == 128 and head_dim % 128 == 0 and positions <= 128


def fused(
    queries,
    keys,
    values,
    history,
    levels,
    patch_two,
    patch_four,
    patch_sixteen,
    mod_scale,
    mod_shift,
    kv_weight,
    key_gain,
):
    n = lax.axis_size("seq")
    tok, width = queries.shape
    hd = key_gain.shape[0]
    per = width // hd // n
    channels, positions = history.shape
    model = mod_scale.shape[0]
    rows = 17 * positions * n // 64
    padded = -(-rows // 32) * 32
    off4 = patch_two.shape[0]
    off16 = -(-(off4 + patch_four.shape[0]) // 128) * 128
    depth = off16 + patch_sixteen.shape[0]
    dims = (n, per, hd, rows, padded, positions, channels, off4, off16)
    bf = jnp.bfloat16
    dma = pltpu.SemaphoreType.DMA
    vmem = pl.BlockSpec(memory_space=pltpu.VMEM)
    anywhere = pl.BlockSpec(memory_space=pl.ANY)
    return pl.pallas_call(
        functools.partial(joint_kernel, dims),
        out_shape=jax.ShapeDtypeStruct((tok, width), bf),
        in_specs=[pl.BlockSpec(memory_space=pltpu.SMEM)] + [vmem] * 4 + [anywhere] * 7,
        out_specs=anywhere,
        scratch_shapes=[
            pltpu.VMEM((n, channels, 128), bf),
            pltpu.VMEM((depth, model), bf),
            pltpu.VMEM(kv_weight.shape, bf),
            pltpu.VMEM((n * positions, depth), bf),
            pltpu.VMEM((padded, model), bf),
            pltpu.VMEM((n, padded // 2, 128), bf),
            pltpu.VMEM((n, padded // 2, 128), bf),
            pltpu.VMEM((n, tok, per * hd), bf),
            pltpu.VMEM((n * tok + padded, per * hd), bf),
            pltpu.VMEM((n * tok + padded, per * hd), bf),
            pltpu.VMEM((n, tok, per * hd), bf),
            dma((4,)),
            dma((4,)),
            dma((n,)),
            dma((n,)),
            dma((n,)),
            dma((n,)),
            dma((2, n)),
            dma((2, n)),
            dma((n,)),
            dma((n,)),
            dma((n,)),
            dma((n,)),
        ],
        compiler_params=pltpu.CompilerParams(
            collective_id=0, has_side_effects=True, vmem_limit_bytes=48 * 2**20
        ),
    )(
        levels,
        history,
        mod_scale.reshape(1, -1),
        mod_shift.reshape(1, -1),
        key_gain.reshape(1, -1),
        queries,
        keys,
        values,
        patch_two,
        patch_four,
        patch_sixteen,
        kv_weight,
    )


def route(*args):
    queries, history, key_gain = args[0], args[3], args[11]
    groups = lax.axis_size("seq")
    chosen = fits_kernel(groups, *queries.shape, key_gain.shape[0], history.shape[1])
    return (fused if chosen else shards)(*args)


def solution(mesh):
    return jax.shard_map(
        route,
        mesh=mesh,
        in_specs=(
            P(("video", "seq"), None),
            P(("video", "seq"), None),
            P(("video", "seq"), None),
            P(None, ("video", "seq")),
            P("video"),
            P(),
            P(),
            P(),
            P(),
            P(),
            P(None, "seq"),
            P(),
        ),
        out_specs=P(("video", "seq"), None),
        check_vma=False,
    )
```

```python
import functools

import jax
import jax.numpy as jnp
from jax import lax
from jax.experimental import pallas as pl
from jax.experimental.pallas import tpu as pltpu
from jax.sharding import PartitionSpec as P

EPS = 1e-06


def divisor_near(total, target):
    parts = max(1, -(-total // target))
    while total % parts != 0:
        parts += 1
    return parts


def key_normed(pairs, gain):
    first = pairs[..., 0, :].astype(jnp.float32)
    scaled = first * lax.rsqrt(jnp.mean(first * first, axis=-1, keepdims=True) + EPS) * gain
    return jnp.concatenate([scaled.astype(jnp.bfloat16), pairs[..., 1, :]], axis=-1)


def level_tokens(everything, weight, level):
    channels, width = everything.shape
    grouped = (
        everything.reshape(channels, width // level, level)
        .transpose(1, 0, 2)
        .reshape(width // level, channels * level)
    )
    return jnp.dot(grouped, weight, preferred_element_type=jnp.float32).astype(jnp.bfloat16)


def history_rows(levels, positions):
    groups = levels.shape[0]
    counts = positions // levels
    before = jnp.arange(groups)[None, :] <= jnp.arange(groups)[:, None]
    ends = jnp.sum(jnp.where(before, counts[None, :], 0), axis=1)
    starts = ends - counts
    block_ids = jnp.arange(groups, dtype=jnp.int32)
    rows_total = 17 * positions * groups // 64
    place = jnp.arange(rows_total, dtype=jnp.int32)
    owner = jnp.sum((ends[None, :] <= place[:, None]).astype(jnp.int32), axis=1)
    match = owner[:, None] == block_ids[None, :]
    inner = place - jnp.sum(jnp.where(match, starts[None, :], 0), axis=1)
    live = jnp.ones((rows_total,), bool)
    level = jnp.sum(jnp.where(match, levels[None, :], 0), axis=1)
    return (owner, inner, level, live)


def attend(query, sec_keys, sec_values, hist_keys, hist_values, live, scale):
    count, size = query.shape
    sources, each, _ = sec_keys.shape
    key_parts = divisor_near(sources, max(1, 2048 // each))
    key_blocks = sec_keys.reshape(key_parts, sources // key_parts * each, size)
    value_blocks = sec_values.reshape(key_parts, sources // key_parts * each, size)
    query_parts = divisor_near(count, 512)
    query_blocks = query.reshape(query_parts, count // query_parts, size)

    def one_block(block):
        scores = jnp.dot(block, hist_keys.T, preferred_element_type=jnp.float32) * scale
        scores = jnp.where(live[None, :], scores, -1e30)
        top = jnp.max(scores, axis=1, keepdims=True)
        weights = jnp.where(live[None, :], jnp.exp(scores - top), 0.0)
        total = jnp.sum(weights, axis=1, keepdims=True)
        acc = jnp.dot(weights.astype(jnp.bfloat16), hist_values, preferred_element_type=jnp.float32)

        def step(carry, pair):
            top_now, total_now, acc_now = carry
            key_block, value_block = pair
            fresh = jnp.dot(block, key_block.T, preferred_element_type=jnp.float32) * scale
            newer = jnp.maximum(top_now, jnp.max(fresh, axis=1, keepdims=True))
            fade = jnp.exp(top_now - newer)
            weights_now = jnp.exp(fresh - newer)
            total_next = total_now * fade + jnp.sum(weights_now, axis=1, keepdims=True)
            acc_next = acc_now * fade + jnp.dot(
                weights_now.astype(jnp.bfloat16), value_block, preferred_element_type=jnp.float32
            )
            return ((newer, total_next, acc_next), None)

        (top, total, acc), _ = lax.scan(step, (top, total, acc), (key_blocks, value_blocks))
        return (acc / total).astype(jnp.bfloat16)

    return lax.map(one_block, query_blocks).reshape(count, size)


def shards(
    queries,
    keys,
    values,
    history,
    levels,
    patch_two,
    patch_four,
    patch_sixteen,
    mod_scale,
    mod_shift,
    kv_weight,
    key_gain,
):
    groups = lax.axis_size("seq")
    device = lax.axis_index("seq")
    tok_dev, width = queries.shape
    head_dim = key_gain.shape[0]
    heads = width // head_dim
    q_split = max(groups // heads, 1)
    per_group = max(heads // groups, 1)
    head_groups = heads // per_group
    q_rows = tok_dev // q_split
    positions = history.shape[1]
    scale = head_dim ** (-0.5)
    everything = lax.all_gather(history, "seq", axis=1, tiled=True)
    owner, inner, level, live = history_rows(levels, positions)
    tokens_two = level_tokens(everything, patch_two, 2)
    tokens_four = level_tokens(everything, patch_four, 4)
    tokens_sixteen = level_tokens(everything, patch_sixteen, 16)
    rows_total = owner.shape[0]
    row_parts = divisor_near(rows_total, 512)

    def project(index):
        own, inn, lev = index
        pick_two = jnp.take(
            tokens_two, own * (positions // 2) + jnp.minimum(inn, positions // 2 - 1), axis=0
        )
        pick_four = jnp.take(
            tokens_four, own * (positions // 4) + jnp.minimum(inn, positions // 4 - 1), axis=0
        )
        pick_sixteen = jnp.take(
            tokens_sixteen, own * (positions // 16) + jnp.minimum(inn, positions // 16 - 1), axis=0
        )
        hidden = jnp.where(
            (lev == 2)[:, None], pick_two, jnp.where((lev == 4)[:, None], pick_four, pick_sixteen)
        )
        feats = hidden.astype(jnp.float32)
        mean = jnp.mean(feats, axis=1, keepdims=True)
        centered = feats - mean
        var = jnp.mean(centered * centered, axis=1, keepdims=True)
        normed = (centered * lax.rsqrt(var + EPS) * (1.0 + mod_scale) + mod_shift).astype(
            jnp.bfloat16
        )
        return jnp.dot(normed, kv_weight, preferred_element_type=jnp.float32).astype(jnp.bfloat16)

    share = lax.map(
        project,
        (owner.reshape(row_parts, -1), inner.reshape(row_parts, -1), level.reshape(row_parts, -1)),
    )
    share = share.reshape(rows_total, kv_weight.shape[1])
    pairs = jnp.concatenate(
        [
            keys.reshape(tok_dev, head_groups, per_group, head_dim),
            values.reshape(tok_dev, head_groups, per_group, head_dim),
        ],
        axis=-1,
    )
    full = lax.all_gather(share, "seq", axis=1, tiled=True)
    ordered = full.reshape(rows_total, head_dim, 2, heads).transpose(0, 3, 2, 1)
    mine = lax.dynamic_index_in_dim(
        ordered.reshape(rows_total, head_groups, per_group, 2, head_dim),
        device // q_split,
        axis=1,
        keepdims=False,
    )
    history_kv = key_normed(mine, key_gain)
    rows_each = pairs.shape[0]
    outgoing = jnp.broadcast_to(
        pairs.transpose(1, 0, 2, 3)[:, None],
        (head_groups, q_split, rows_each, per_group, 2 * head_dim),
    )
    outgoing = outgoing.reshape(groups, rows_each, per_group * 2 * head_dim)
    sending = (
        queries.reshape(q_split, q_rows, head_groups, per_group * head_dim)
        .transpose(2, 0, 1, 3)
        .reshape(groups, q_rows, per_group * head_dim)
    )
    got_queries, got_pairs = (
        lax.all_to_all(sending, "seq", split_axis=0, concat_axis=0, tiled=True),
        lax.all_to_all(outgoing, "seq", split_axis=0, concat_axis=0, tiled=True),
    )
    results = []
    for item in range(per_group):
        query = got_queries[:, :, item * head_dim : (item + 1) * head_dim].reshape(
            groups * q_rows, head_dim
        )
        base = item * 2 * head_dim
        sec_keys = got_pairs[:, :, base : base + head_dim]
        sec_values = got_pairs[:, :, base + head_dim : base + 2 * head_dim]
        hist_keys = history_kv[:, item, :head_dim]
        hist_values = history_kv[:, item, head_dim:]
        results.append(attend(query, sec_keys, sec_values, hist_keys, hist_values, live, scale))
    mixed = jnp.concatenate(results, axis=-1).reshape(groups, q_rows, per_group * head_dim)
    returned = lax.all_to_all(mixed, "seq", split_axis=0, concat_axis=0, tiled=True)
    return (
        returned.reshape(head_groups, q_split, q_rows, per_group * head_dim)
        .transpose(1, 2, 0, 3)
        .reshape(tok_dev, width)
    )


def joint_kernel(
    dims,
    levels_ref,
    history_ref,
    scale_ref,
    shift_ref,
    gain_ref,
    queries_ref,
    keys_ref,
    values_ref,
    two_ref,
    four_ref,
    sixteen_ref,
    weight_ref,
    out_ref,
    raw,
    patches,
    weight,
    spread,
    hidden,
    share_out,
    share_in,
    qbuf,
    kbuf,
    vbuf,
    obuf,
    load_sem,
    own_sem,
    hist_send,
    hist_recv,
    share_send,
    share_recv,
    kv_send,
    kv_recv,
    q_send,
    q_recv,
    o_send,
    o_recv,
):
    n, per, hd, rows, padded, positions, channels, off4, off16 = dims
    tok = queries_ref.shape[0]
    wide = per * hd
    half = padded // 2
    heads = n * per
    chan = hd // n
    kinds = 2 * per
    model = hidden.shape[1]
    bf, f32 = jnp.bfloat16, jnp.float32
    me = lax.axis_index("seq")

    def partner(i):
        return n // 2 + (1 - 2 * (i % 2)) * (i // 2)

    def target(i):
        return lax.rem(me + partner(i), n)

    def origin(i):
        return lax.rem(me + n - partner(i), n)

    def lanes(index):
        return pl.ds(pl.multiple_of(index * wide, 128), wide)

    def band(index):
        return pl.ds(pl.multiple_of(index * tok, 16), tok)

    def remote(src, dst, send, recv, device):
        return pltpu.make_async_remote_copy(
            src_ref=src,
            dst_ref=dst,
            send_sem=send,
            recv_sem=recv,
            device_id={"seq": device},
            device_id_type=pl.DeviceIdType.MESH,
        )

    def hist_copy(device, source):
        return remote(
            raw.at[source], raw.at[source], hist_send.at[device], hist_recv.at[source], device
        )

    def key_copy(device, source):
        return remote(
            keys_ref.at[:, lanes(device)],
            kbuf.at[band(source), :],
            kv_send.at[0, device],
            kv_recv.at[0, source],
            device,
        )

    def value_copy(device, source):
        return remote(
            values_ref.at[:, lanes(device)],
            vbuf.at[band(source), :],
            kv_send.at[1, device],
            kv_recv.at[1, source],
            device,
        )

    def query_copy(device, source):
        return remote(
            queries_ref.at[:, lanes(device)],
            qbuf.at[source],
            q_send.at[device],
            q_recv.at[source],
            device,
        )

    def share_copy(device, source):
        return remote(
            share_out.at[device],
            share_in.at[source],
            share_send.at[device],
            share_recv.at[source],
            device,
        )

    def out_copy(device, source):
        return remote(
            obuf.at[device],
            out_ref.at[:, lanes(source)],
            o_send.at[device],
            o_recv.at[source],
            device,
        )

    n2, n4, n16 = two_ref.shape[0], four_ref.shape[0], sixteen_ref.shape[0]
    loads = [
        pltpu.make_async_copy(two_ref, patches.at[pl.ds(0, n2), :], load_sem.at[0]),
        pltpu.make_async_copy(four_ref, patches.at[pl.ds(off4, n4), :], load_sem.at[1]),
        pltpu.make_async_copy(sixteen_ref, patches.at[pl.ds(off16, n16), :], load_sem.at[2]),
        pltpu.make_async_copy(weight_ref, weight, load_sem.at[3]),
    ]
    own = [
        pltpu.make_async_copy(keys_ref.at[:, lanes(me)], kbuf.at[band(me), :], own_sem.at[0]),
        pltpu.make_async_copy(values_ref.at[:, lanes(me)], vbuf.at[band(me), :], own_sem.at[1]),
        pltpu.make_async_copy(queries_ref.at[:, lanes(me)], qbuf.at[me], own_sem.at[2]),
    ]

    barrier = pltpu.get_barrier_semaphore()

    @pl.loop(1, n)
    def _(i):
        pl.semaphore_signal(
            barrier, inc=1, device_id={"seq": target(i)}, device_id_type=pl.DeviceIdType.MESH
        )

    for copy in loads + own:
        copy.start()
    gap = off16 - off4 - n4
    if gap:
        patches[off4 + n4 : off16, :] = jnp.zeros((gap, model), bf)
    raw[me] = jnp.concatenate(
        [history_ref[...], jnp.zeros((channels, 128 - positions), bf)], axis=1
    )
    pl.semaphore_wait(barrier, n - 1)

    @pl.loop(1, n)
    def _(i):
        hist_copy(target(i), me).start()

    @pl.loop(1, n)
    def _(i):
        key_copy(target(i), me).start()
        value_copy(target(i), me).start()

    spots = n * positions
    row = lax.broadcasted_iota(jnp.int32, (padded, spots), 0)
    spot = lax.broadcasted_iota(jnp.int32, (1, spots), 1)
    start = jnp.int32(0)
    first = jnp.zeros((1, spots), jnp.int32)
    factor = jnp.ones((1, spots), jnp.int32)
    block_levels = []
    for b in range(n):
        level = levels_ref[b]
        block_levels.append(level)
        inside = spot // positions == b
        first = jnp.where(inside, start, first)
        factor = jnp.where(inside, level, factor)
        start = start + jnp.where(
            level == 2, positions // 2, jnp.where(level == 4, positions // 4, positions // 16)
        )
    begin = (row - first) * factor
    local = spot % positions
    member = jnp.where((begin <= local) & (local < begin + factor), 1.0, 0.0).astype(bf)

    width = patches.shape[0]
    column = lax.broadcasted_iota(jnp.int32, (1, width), 1)
    kind = jnp.where(
        column < off4,
        2,
        jnp.where(column < off4 + n4, 4, jnp.where(column < off16, 1, 16)),
    )
    base = jnp.where(column < off4, 0, jnp.where(column < off16, off4, off16))
    within = column - base
    owner_channel = jnp.where(
        kind == 2, within // 2, jnp.where(kind == 4, within // 4, within // 16)
    )
    phase = within - owner_channel * kind
    channel = lax.broadcasted_iota(jnp.int32, (channels, width), 0)
    expand = jnp.where((channel == owner_channel) & (kind > 1), 1.0, 0.0).astype(bf)
    at = lax.broadcasted_iota(jnp.int32, (128, width), 0)
    remainder = jnp.where(kind == 2, at % 2, jnp.where(kind == 4, at % 4, at % 16))
    fits = remainder == phase

    @pl.loop(1, n)
    def _(i):
        hist_copy(origin(i), origin(i)).wait_recv()

    for b in range(n):
        spreaded = lax.dot_general(
            raw[b], expand, (((0,), (0,)), ((), ())), preferred_element_type=f32
        )
        keep = fits & (kind == block_levels[b])
        spread[b * positions : (b + 1) * positions, :] = jnp.where(keep, spreaded, 0.0).astype(bf)[
            :positions
        ]
    grouped = jnp.dot(member, spread[...], preferred_element_type=f32).astype(bf)
    for copy in loads[:3]:
        copy.wait()
    step = 512 if model % 512 == 0 else model
    total = jnp.zeros((padded, 1), f32)
    for c in range(0, model, step):
        tokens = jnp.dot(
            grouped, patches[:, c : c + step], preferred_element_type=f32
        ).astype(bf)
        hidden[:, c : c + step] = tokens
        total = total + jnp.sum(tokens.astype(f32), axis=1, keepdims=True)
    mean = total / model
    square = jnp.zeros((padded, 1), f32)
    for c in range(0, model, step):
        centered = hidden[:, c : c + step].astype(f32) - mean
        square = square + jnp.sum(centered * centered, axis=1, keepdims=True)
    inverse = lax.rsqrt(square / model + EPS)
    loads[3].wait()
    projected = jnp.zeros((padded, weight.shape[1]), f32)
    for c in range(0, model, step):
        centered = hidden[:, c : c + step].astype(f32) - mean
        normed = (
            centered * inverse * (1.0 + scale_ref[:, c : c + step]) + shift_ref[:, c : c + step]
        ).astype(bf)
        projected = projected + jnp.dot(
            normed, weight[c : c + step, :], preferred_element_type=f32
        )
    share = projected.astype(bf)

    cols = chan * 2 * heads
    take = lax.broadcasted_iota(jnp.int32, (cols, n * 128), 0)
    give = lax.broadcasted_iota(jnp.int32, (1, n * 128), 1)
    lane = give % (kinds * chan)
    dest = give // 128
    which = lane // chan
    wanted = (lane % chan) * 2 * heads + (which // per) * heads + dest * per + which % per
    order = jnp.where(take == wanted, 1.0, 0.0).astype(bf)
    low = jnp.dot(share[:half], order, preferred_element_type=f32)
    high = jnp.dot(share[half:], order, preferred_element_type=f32)
    both = jnp.where(give % 128 < kinds * chan, low, high).astype(bf)
    for g in range(n):
        share_out[g] = both[:, g * 128 : (g + 1) * 128]

    @pl.loop(1, n)
    def _(i):
        share_copy(target(i), me).start()

    @pl.loop(1, n)
    def _(i):
        query_copy(target(i), me).start()

    share_in[me] = share_out[me]
    taking = lax.broadcasted_iota(jnp.int32, (128, kinds * hd), 0)
    giving = lax.broadcasted_iota(jnp.int32, (1, kinds * hd), 1)
    in_head = giving % hd
    lane_of = (giving // hd) * chan + in_head % chan

    @pl.loop(1, n)
    def _(i):
        share_copy(origin(i), origin(i)).wait_recv()

    low = jnp.zeros((half, kinds * hd), f32)
    high = jnp.zeros((half, kinds * hd), f32)
    for s in range(n):
        from_s = in_head // chan == s
        put_low = jnp.where((taking == lane_of) & from_s, 1.0, 0.0).astype(bf)
        put_high = jnp.where((taking == lane_of + kinds * chan) & from_s, 1.0, 0.0).astype(bf)
        low = low + jnp.dot(share_in[s], put_low, preferred_element_type=f32)
        high = high + jnp.dot(share_in[s], put_high, preferred_element_type=f32)
    gathered = jnp.concatenate([low, high], axis=0)
    section = n * tok
    for h in range(per):
        key = gathered[:, h * hd : (h + 1) * hd]
        norm = lax.rsqrt(jnp.mean(key * key, axis=1, keepdims=True) + EPS)
        kbuf[section:, h * hd : (h + 1) * hd] = (key * norm * gain_ref[...]).astype(bf)
        vbuf[section:, h * hd : (h + 1) * hd] = gathered[
            :, (per + h) * hd : (per + h + 1) * hd
        ].astype(bf)

    for copy in own:
        copy.wait()

    @pl.loop(1, n)
    def _(i):
        key_copy(origin(i), origin(i)).wait_recv()
        value_copy(origin(i), origin(i)).wait_recv()

    rate = hd**-0.5 * 1.4426950408889634
    live = lax.broadcasted_iota(jnp.int32, (1, padded), 1) < rows
    across = (((1,), (1,)), ((), ()))

    def attend_block(source):
        for h in range(per):
            cut = slice(h * hd, (h + 1) * hd)
            query = qbuf[source, :, cut]
            near = lax.dot_general(query, kbuf[:section, cut], across, preferred_element_type=f32)
            past = lax.dot_general(query, kbuf[section:, cut], across, preferred_element_type=f32)
            past = jnp.where(live, past, -1e30)
            top = jnp.maximum(
                jnp.max(near, axis=1, keepdims=True), jnp.max(past, axis=1, keepdims=True)
            )
            near = jnp.exp2((near - top) * rate)
            past = jnp.exp2((past - top) * rate)
            total = jnp.sum(near, axis=1, keepdims=True) + jnp.sum(past, axis=1, keepdims=True)
            mixed = jnp.dot(near.astype(bf), vbuf[:section, cut], preferred_element_type=f32)
            mixed = mixed + jnp.dot(past.astype(bf), vbuf[section:, cut], preferred_element_type=f32)
            obuf[source, :, cut] = (mixed / total).astype(bf)

    attend_block(me)
    own_out = pltpu.make_async_copy(obuf.at[me], out_ref.at[:, lanes(me)], own_sem.at[3])
    own_out.start()

    @pl.loop(1, n)
    def _(i):
        source = origin(i)
        query_copy(source, source).wait_recv()
        attend_block(source)
        out_copy(source, me).start()

    @pl.loop(1, n)
    def _(i):
        device = target(i)
        hist_copy(device, me).wait_send()
        key_copy(device, me).wait_send()
        value_copy(device, me).wait_send()
        share_copy(device, me).wait_send()
        query_copy(device, me).wait_send()
        out_copy(device, me).wait_send()

    @pl.loop(1, n)
    def _(i):
        out_copy(origin(i), origin(i)).wait_recv()

    own_out.wait()


def fits_kernel(groups, tok_dev, width, head_dim, positions):
    heads = width // head_dim
    if groups < 2 or groups % 2 or heads % groups or head_dim % groups or tok_dev % 16:
        return False
    per_group = heads // groups
    held = 4 * 2 * groups * tok_dev * per_group * head_dim
    lanes = 4 * per_group * (head_dim // groups)
    return held <= 16 * 2**20 and lanes == 128 and head_dim % 128 == 0 and positions <= 128


def fused(
    queries,
    keys,
    values,
    history,
    levels,
    patch_two,
    patch_four,
    patch_sixteen,
    mod_scale,
    mod_shift,
    kv_weight,
    key_gain,
):
    n = lax.axis_size("seq")
    tok, width = queries.shape
    hd = key_gain.shape[0]
    per = width // hd // n
    channels, positions = history.shape
    model = mod_scale.shape[0]
    rows = 17 * positions * n // 64
    padded = -(-rows // 32) * 32
    off4 = patch_two.shape[0]
    off16 = -(-(off4 + patch_four.shape[0]) // 128) * 128
    depth = off16 + patch_sixteen.shape[0]
    dims = (n, per, hd, rows, padded, positions, channels, off4, off16)
    bf = jnp.bfloat16
    dma = pltpu.SemaphoreType.DMA
    vmem = pl.BlockSpec(memory_space=pltpu.VMEM)
    anywhere = pl.BlockSpec(memory_space=pltpu.HBM)
    return pl.pallas_call(
        functools.partial(joint_kernel, dims),
        out_shape=jax.ShapeDtypeStruct((tok, width), bf),
        in_specs=[pl.BlockSpec(memory_space=pltpu.SMEM)] + [vmem] * 4 + [anywhere] * 7,
        out_specs=anywhere,
        scratch_shapes=[
            pltpu.VMEM((n, channels, 128), bf),
            pltpu.VMEM((depth, model), bf),
            pltpu.VMEM(kv_weight.shape, bf),
            pltpu.VMEM((n * positions, depth), bf),
            pltpu.VMEM((padded, model), bf),
            pltpu.VMEM((n, padded // 2, 128), bf),
            pltpu.VMEM((n, padded // 2, 128), bf),
            pltpu.VMEM((n, tok, per * hd), bf),
            pltpu.VMEM((n * tok + padded, per * hd), bf),
            pltpu.VMEM((n * tok + padded, per * hd), bf),
            pltpu.VMEM((n, tok, per * hd), bf),
            dma((4,)),
            dma((4,)),
            dma((n,)),
            dma((n,)),
            dma((n,)),
            dma((n,)),
            dma((2, n)),
            dma((2, n)),
            dma((n,)),
            dma((n,)),
            dma((n,)),
            dma((n,)),
        ],
        compiler_params=pltpu.CompilerParams(
            collective_id=0, has_side_effects=True, vmem_limit_bytes=63 * 2**20
        ),
    )(
        levels,
        history,
        mod_scale.reshape(1, -1),
        mod_shift.reshape(1, -1),
        key_gain.reshape(1, -1),
        queries,
        keys,
        values,
        patch_two,
        patch_four,
        patch_sixteen,
        kv_weight,
    )


def route(*args):
    queries, history, key_gain = args[0], args[3], args[11]
    groups = lax.axis_size("seq")
    chosen = fits_kernel(groups, *queries.shape, key_gain.shape[0], history.shape[1])
    return (fused if chosen else shards)(*args)


def solution(mesh):
    return jax.shard_map(
        route,
        mesh=mesh,
        in_specs=(
            P(("video", "seq"), None),
            P(("video", "seq"), None),
            P(("video", "seq"), None),
            P(None, ("video", "seq")),
            P("video"),
            P(),
            P(),
            P(),
            P(),
            P(),
            P(None, "seq"),
            P(),
        ),
        out_specs=P(("video", "seq"), None),
        check_vma=False,
    )
```
